32 devices in a mesh: row: 8 (over y, x, core), col: 4 (over z).
Axes of the slice: x: 2, y: 2, z: 4, core: 2. Of those that a mesh axis runs over, the one named last changes fastest.
Arguments:
- latent: bfloat16 [672, 672, 256], P('row', 'col'), may hold values from -6 to 6
- cotangent: bfloat16 [672, 672, 256], P('row', 'col'), may hold values from -6 to 6
- factor_one: bfloat16 [672, 672], P('row'), as said below
- factor_two: bfloat16 [672, 672], P('col'), as said below
Outputs:
- grad_latent: bfloat16 [672, 672, 256], P('row', 'col')
- grad_factor_one: float32 [672, 672], P('row', 'col')
- grad_factor_two: float32 [672, 672], P('row', 'col')
The draws below stay inside these ranges and needn't reach their ends.
Inputs may be any that keep to these rules, and one draw needn't show every extreme that they name: `factor_one`: lower triangular, with diagonal entries between 0.5 and 1.5. `factor_two`: lower triangular, with diagonal entries between 0.5 and 1.5.
All inputs are finite; a program needn't handle non-finite values.
Results may differ from the reference program's by a relative error of at most 0.0049.
Values may be sent and summed in bfloat16 or wider, within the bound.
No kernel may reach another device: no remote copies, remote signals or barrier semaphores. Data moves between devices by JAX's collectives and lax.ppermute only.
A program may use at most 128 MiB of HBM per device.

```python
import math
import jax
import jax.numpy as jnp
from jax import lax

N1 = 672
N2 = 672
K = 256


def lower_factor(key, order):
    first, second = jax.random.split(key)
    diagonal = jax.random.uniform(first, (order,), jnp.float32, 0.5, 1.5)
    below = jnp.clip(jax.random.normal(second, (order, order), jnp.float32), -4.0, 4.0) / math.sqrt(order)
    row_ids = lax.broadcasted_iota(jnp.int32, (order, order), 0)
    col_ids = lax.broadcasted_iota(jnp.int32, (order, order), 1)
    strict = jnp.where(row_ids > col_ids, below, 0.0)
    on_diag = jnp.where(row_ids == col_ids, diagonal[None, :], 0.0)
    return strict + on_diag


def draw_factor_one(key, part):
    return lower_factor(jax.random.fold_in(key, 11), N1).astype(jnp.bfloat16)


def draw_factor_two(key, part):
    return lower_factor(jax.random.fold_in(key, 23), N2).astype(jnp.bfloat16)


def steps_of(key, shape, cuts, least, top_value):
    loudness, own = 1.0, jax.random.fold_in(key, 6)
    for dim, parts in cuts:
        draws = jnp.exp(jax.random.uniform(jax.random.fold_in(own, dim), (parts,), jnp.float32, least / len(cuts), top_value / len(cuts)))
        loudness = loudness * jnp.repeat(draws, shape[dim] // parts).reshape([-1 if axis == dim else 1 for axis in range(len(shape))])
    return loudness


def gaussian(rng, dims, scale, most, pieces=(), held_as=jnp.bfloat16):
    factor_of = steps_of(rng, dims, pieces, -0.22, 0.18) if pieces else 1.0
    values = jax.random.normal(rng, dims, jnp.float32) * scale * factor_of
    return jnp.minimum(jnp.maximum(values, -most), most).astype(held_as)


def setup_inputs(seed: int = 0) -> dict:
    key_list = jax.random.split(jax.random.key(seed), 5)
    return {
        "latent": gaussian(key_list[0], (N1, N2, K), 1.0, 6.0, ((0, 8), (1, 4))),
        "cotangent": gaussian(key_list[1], (N1, N2, K), 1.0, 6.0, ((0, 8), (1, 4))),
        "factor_one": draw_factor_one(jax.random.fold_in(key_list[4], 71), 0),
        "factor_two": draw_factor_two(jax.random.fold_in(key_list[4], 71), 0),
    }


def reference(latent, cotangent, factor_one, factor_two):
    width = math.gcd(K, 32)
    count = K // width
    high = lax.Precision.HIGHEST
    left = factor_one.astype(jnp.float32)
    right = factor_two.astype(jnp.float32)
    latent_blocks = latent.reshape(N1, N2, count, width).transpose(2, 0, 1, 3)
    cotan_blocks = cotangent.reshape(N1, N2, count, width).transpose(2, 0, 1, 3)

    def advance(carry, pair):
        sum_one, sum_two = carry
        field = pair[0].astype(jnp.float32)
        incoming = pair[1].astype(jnp.float32)
        mixed = jnp.einsum('jb,abk->ajk', right, field, precision=high).astype(jnp.bfloat16)
        mixed = lax.optimization_barrier(mixed).astype(jnp.float32)
        pulled = jnp.einsum('ia,ijk->ajk', left, incoming, precision=high).astype(jnp.bfloat16)
        pulled = lax.optimization_barrier(pulled).astype(jnp.float32)
        sum_one = sum_one + jnp.einsum('ijk,ajk->ia', incoming, mixed, precision=high)
        sum_two = sum_two + jnp.einsum('ajk,abk->jb', pulled, field, precision=high)
        result = jnp.einsum('jb,ajk->abk', right, pulled, precision=high).astype(jnp.bfloat16)
        return (sum_one, sum_two), result

    start = (jnp.zeros((N1, N1), jnp.float32), jnp.zeros((N2, N2), jnp.float32))
    (sum_one, sum_two), results = lax.scan(advance, start, (latent_blocks, cotan_blocks))
    grad_latent = results.transpose(1, 2, 0, 3).reshape(N1, N2, K)
    return grad_latent, jnp.tril(sum_one) / K, jnp.tril(sum_two) / K
```

```python
import functools

import jax
import jax.numpy as jnp
from jax import lax
from jax.experimental import pallas as pl
from jax.experimental.pallas import tpu as pltpu
from jax.sharding import PartitionSpec as P

LANES = 128
F32, BF16 = jnp.float32, jnp.bfloat16


def contract_first(left, right):
    return lax.dot_general(
        left, right, (((0,), (0,)), ((), ())), preferred_element_type=F32
    )


def contract_last(left, right):
    return lax.dot_general(
        left, right, (((1,), (1,)), ((), ())), preferred_element_type=F32
    )


def keep_lower(portion, depth):
    span_rows, span_cols = portion.shape
    row_ids = lax.axis_index("row") * span_rows + lax.broadcasted_iota(
        jnp.int32, (span_rows, span_cols), 0
    )
    col_ids = lax.axis_index("col") * span_cols + lax.broadcasted_iota(
        jnp.int32, (span_rows, span_cols), 1
    )
    return jnp.where(row_ids >= col_ids, portion / depth, 0.0)


def reduce_grad(partial_value, depth):
    portion = lax.psum_scatter(partial_value, "row", scatter_dimension=0, tiled=True)
    portion = lax.psum_scatter(portion, "col", scatter_dimension=1, tiled=True)
    return keep_lower(portion, depth)


def by_lines(latent, cotangent, factor_one, factor_two):
    rows_one, rows_two, depth = latent.shape
    latent_flat = jnp.transpose(latent, (1, 0, 2)).reshape(rows_two, rows_one * depth)
    latent_two = lax.all_to_all(latent_flat, "col", split_axis=1, concat_axis=0, tiled=True)
    cotan_flat = cotangent.reshape(rows_one, rows_two * depth)
    cotan_one = lax.all_to_all(cotan_flat, "row", split_axis=1, concat_axis=0, tiled=True)
    full_one = lax.all_gather(factor_one, "row", axis=0, tiled=True)
    full_two = lax.all_gather(factor_two, "col", axis=0, tiled=True)
    mixed_two = jnp.dot(full_two, latent_two, preferred_element_type=F32)
    pulled_one = contract_first(full_one, cotan_one)
    mixed_two = mixed_two.astype(BF16)
    pulled_one = pulled_one.astype(BF16)
    mixed_back = lax.all_to_all(mixed_two, "col", split_axis=0, concat_axis=1, tiled=True)
    mixed_block = (
        mixed_back.reshape(rows_two, rows_one, depth)
        .transpose(1, 0, 2)
        .reshape(rows_one, rows_two * depth)
    )
    mixed_one = lax.all_to_all(mixed_block, "row", split_axis=1, concat_axis=0, tiled=True)
    pulled_back = lax.all_to_all(pulled_one, "row", split_axis=0, concat_axis=1, tiled=True)
    pulled_block = (
        pulled_back.reshape(rows_one, rows_two, depth)
        .transpose(1, 0, 2)
        .reshape(rows_two, rows_one * depth)
    )
    pulled_two = lax.all_to_all(pulled_block, "col", split_axis=1, concat_axis=0, tiled=True)
    grad_factor_one = reduce_grad(contract_last(cotan_one, mixed_one), depth)
    grad_factor_two = reduce_grad(contract_last(pulled_two, latent_two), depth)
    result_two = contract_first(full_two, pulled_two)
    result_two = result_two.astype(BF16)
    result_back = lax.all_to_all(result_two, "col", split_axis=0, concat_axis=1, tiled=True)
    grad_latent = result_back.reshape(rows_two, rows_one, depth).transpose(1, 0, 2)
    return (grad_latent, grad_factor_one, grad_factor_two)


def dot(left, right):
    return jnp.dot(left, right, preferred_element_type=F32)


def dot_nt(left, right):
    return lax.dot_general(
        left, right, (((1,), (1,)), ((), ())), preferred_element_type=F32
    )


def whole(shape):
    return pl.BlockSpec(shape, lambda *_: (0,) * len(shape))


def params():
    return pltpu.CompilerParams(vmem_limit_bytes=48 * 1024 * 1024)


def cost(flops, arrays):
    return pl.CostEstimate(flops=1, bytes_accessed=1, transcendentals=0)


def swap_matrix(fold):
    size = fold * LANES
    part = LANES // fold
    rows = lax.broadcasted_iota(jnp.int32, (size, size), 0)
    cols = lax.broadcasted_iota(jnp.int32, (size, size), 1)
    major, minor, lane = rows // LANES, (rows % LANES) // part, rows % part
    return (cols == minor * LANES + major * part + lane).astype(BF16)


def lanes_of(pieces):
    return jnp.concatenate(pieces, axis=-1)


def group(value, index):
    return value[:, index * LANES : (index + 1) * LANES]


HELD = pl.BlockSpec(memory_space=pl.ANY)


def pack(block, swap, tiles, span, rows):
    depth = block.shape[2]
    fold = swap.shape[0] // LANES
    first, count = tiles[0], tiles[1] - tiles[0]
    lo, hi = span
    wide_rows = hi - lo if lo % (hi - lo) == 0 else lo
    per = 3 if first % 3 == 0 and count % 3 == 0 else 1

    def kernel(x_ref, p_ref, o_ref):
        for t in range(per):
            for half in range(depth // LANES):
                at = half * LANES
                x = lanes_of([x_ref[t * fold + n, : hi - lo, at : at + LANES] for n in range(fold)])
                y = dot(x, p_ref[...]).astype(BF16)
                for n in range(fold):
                    o_ref[half * fold + n, t] = group(y, n)

    out = jax.ShapeDtypeStruct((rows, count, hi - lo, LANES), BF16)
    return pl.pallas_call(
        kernel,
        grid=(count // per,),
        in_specs=[
            pl.BlockSpec(
                (per * fold, wide_rows, depth), lambda t: (first // per + t, lo // wide_rows, 0)
            ),
            whole(swap.shape),
        ],
        out_specs=pl.BlockSpec((rows, per, hi - lo, LANES), lambda t: (0, t, 0, 0)),
        out_shape=out,
        compiler_params=params(),
        cost_estimate=cost(2 * out.size * swap.shape[0], (out, out)),
        name="pack",
    )(block, swap)


def unpack(part, swap, shape, where, before):
    rows, tiles, span, _ = part.shape
    fold = swap.shape[0] // LANES
    depth = shape[2]
    lo, hi, unit = where
    index = lo // unit
    extra = [] if before is None else [before]
    per = 3 if tiles % 3 == 0 else 1

    def kernel(x_ref, p_ref, *rest):
        o_ref = rest[-1]
        for t in range(per):
            for half in range(depth // LANES):
                x = lanes_of([x_ref[half * fold + n, t] for n in range(fold)])
                y = dot(x, p_ref[...]).astype(BF16)
                for n in range(fold):
                    at = half * LANES
                    o_ref[t * fold + n, :span, at : at + LANES] = group(y, n)

    return pl.pallas_call(
        kernel,
        grid=(tiles // per,),
        in_specs=[
            pl.BlockSpec((rows, per, span, LANES), lambda t: (0, t, 0, 0)),
            whole(swap.shape),
        ]
        + [HELD] * len(extra),
        out_specs=pl.BlockSpec((per * fold, unit, depth), lambda t: (t, index, 0)),
        out_shape=jax.ShapeDtypeStruct(shape, BF16),
        input_output_aliases={2: 0} if extra else {},
        compiler_params=params(),
        cost_estimate=cost(2 * part.size * swap.shape[0], (part, part)),
        name="unpack",
    )(part, swap, *extra)


def swapped(pieces):
    fold = len(pieces)
    width = LANES // fold
    return [
        lanes_of([x[:, n * width : (n + 1) * width] for x in pieces]) for n in range(fold)
    ]


def to_y(refs, base, fold):
    turned = [swapped([r[base + n].astype(F32) for n in range(fold)]) for r in refs]
    return jnp.concatenate([y[n] for n in range(fold) for y in turned], axis=0).astype(BF16)


def from_y(value, refs, base, fold):
    spans = [r.shape[1] for r in refs]
    total = sum(spans)
    start = 0
    for r, span in zip(refs, spans):
        y = swapped([value[n * total + start : n * total + start + span] for n in range(fold)])
        for n in range(fold):
            r[base + n] = y[n].astype(BF16)
        start += span


def raise_field(field, left, fold, spans):
    span_two = field.shape[0]
    order = left.shape[0]
    step = 2 * fold
    count = span_two // step

    def kernel(x_ref, l_ref, y_ref, *outs):
        y = lanes_of([to_y([x_ref], u * fold, fold) for u in range(2)])
        y_ref[0] = y
        v = dot(l_ref[...], y)
        for u in range(2):
            from_y(group(v, u), outs, u * fold, fold)

    shapes = [jax.ShapeDtypeStruct((span_two, span, LANES), BF16) for span in spans]
    y_shape = jax.ShapeDtypeStruct((count, order, 2 * LANES), BF16)
    return pl.pallas_call(
        kernel,
        grid=(count,),
        in_specs=[pl.BlockSpec((step,) + field.shape[1:], lambda t: (t, 0, 0)), whole(left.shape)],
        out_specs=[pl.BlockSpec((1, order, 2 * LANES), lambda t: (t, 0, 0))]
        + [pl.BlockSpec((step, span, LANES), lambda t: (t, 0, 0)) for span in spans],
        out_shape=[y_shape] + shapes,
        compiler_params=params(),
        cost_estimate=cost(2 * y_shape.size * order, (y_shape,) * 3),
        name="raise_field",
    )(field, left)


def finish(parts, left_t, fold):
    span_two = parts[0].shape[0]
    order = left_t.shape[0]
    step = 2 * fold
    count = span_two // step
    n = len(parts)

    def kernel(*refs):
        ins, l_ref, out_ref, y_ref = refs[:n], refs[n], refs[n + 1], refs[n + 2]
        w = lanes_of([to_y(ins, u * fold, fold) for u in range(2)])
        y_ref[0] = w
        v = dot(l_ref[...], w)
        for u in range(2):
            from_y(group(v, u), [out_ref], u * fold, fold)

    out = jax.ShapeDtypeStruct((span_two, order // fold, LANES), BF16)
    y_shape = jax.ShapeDtypeStruct((count, order, 2 * LANES), BF16)
    return pl.pallas_call(
        kernel,
        grid=(count,),
        in_specs=[pl.BlockSpec((step,) + p.shape[1:], lambda t: (t, 0, 0)) for p in parts]
        + [whole(left_t.shape)],
        out_specs=[
            pl.BlockSpec((step,) + out.shape[1:], lambda t: (t, 0, 0)),
            pl.BlockSpec((1, order, 2 * LANES), lambda t: (t, 0, 0)),
        ],
        out_shape=[out, y_shape],
        compiler_params=params(),
        cost_estimate=cost(2 * out.size * order, (out,) * 3),
        name="finish",
    )(*parts, left_t)


def match(w, z, first, before):
    count, order, width = w.shape
    extra = [] if before is None else [before]

    def kernel(w_ref, z_ref, *rest):
        g_ref = rest[-1]

        @pl.when(pl.program_id(0) == 0)
        def _():
            g_ref[...] = jnp.zeros_like(g_ref) if before is None else rest[0][...]

        g_ref[...] += dot_nt(w_ref[0], z_ref[0])

    g_shape = jax.ShapeDtypeStruct((order, order), F32)
    return pl.pallas_call(
        kernel,
        grid=(count,),
        in_specs=[
            pl.BlockSpec((1, order, width), lambda t: (t, 0, 0)),
            pl.BlockSpec((1, order, width), lambda t: (first + t, 0, 0)),
        ]
        + [whole(b.shape) for b in extra],
        out_specs=whole(g_shape.shape),
        out_shape=g_shape,
        compiler_params=params(),
        cost_estimate=cost(2 * w.size * order, (w, w)),
        name="match",
    )(w, z, *extra)


def wide(ref):
    return lanes_of([ref[t] for t in range(ref.shape[0])])


def tall(refs):
    return jnp.concatenate([wide(r) for r in refs], axis=0)


def gathered(slots, fields, mix, cuts, per):
    tiles, span_two, _ = slots[0].shape
    n, m = len(slots), len(fields)

    def kernel(*refs):
        ins, vs, m_ref = refs[:n], refs[n : n + m], refs[n + m]
        outs, g_ref = refs[n + m + 1 : -1], refs[-1]

        @pl.when(pl.program_id(0) == 0)
        def _():
            g_ref[...] = jnp.zeros_like(g_ref)

        v = tall(vs)
        total = None
        for d in range(n):
            c = wide(ins[d])
            g_ref[d] += dot_nt(c, v)
            term = dot(m_ref[d], c)
            total = term if total is None else total + term
        total = total.astype(BF16)
        for (lo, hi), out in zip(cuts, outs):
            for t in range(per):
                out[t] = group(total[lo:hi], t)

    def spec(span):
        return pl.BlockSpec((per, span, LANES), lambda t: (t, 0, 0))

    g_shape = jax.ShapeDtypeStruct((n, span_two, span_two), F32)
    return pl.pallas_call(
        kernel,
        grid=(tiles // per,),
        in_specs=[spec(span_two)] * n + [spec(f.shape[1]) for f in fields] + [whole(mix.shape)],
        out_specs=[spec(hi - lo) for lo, hi in cuts] + [whole(g_shape.shape)],
        out_shape=[jax.ShapeDtypeStruct((tiles, hi - lo, LANES), BF16) for lo, hi in cuts]
        + [g_shape],
        compiler_params=params(),
        cost_estimate=cost(4 * slots[0].size * n * span_two, tuple(slots) + tuple(slots[:2])),
        name="gathered",
    )(*slots, *fields, mix)


def pairs(field, others, per):
    tiles, span_two, _ = field.shape
    n = len(others)

    def kernel(*refs):
        c_ref, ins, g_ref = refs[0], refs[1 : n + 1], refs[-1]

        @pl.when(pl.program_id(0) == 0)
        def _():
            g_ref[...] = jnp.zeros_like(g_ref)

        g_ref[...] += dot_nt(wide(c_ref), tall(ins))

    def spec(span):
        return pl.BlockSpec((per, span, LANES), lambda t: (t, 0, 0))

    g_shape = jax.ShapeDtypeStruct((span_two, span_two), F32)
    return pl.pallas_call(
        kernel,
        grid=(tiles // per,),
        in_specs=[spec(span_two)] + [spec(o.shape[1]) for o in others],
        out_specs=whole(g_shape.shape),
        out_shape=g_shape,
        compiler_params=params(),
        cost_estimate=cost(2 * field.size * span_two, (field, field)),
        name="pairs",
    )(field, *others)


def shares(field, mix, cuts, per):
    tiles, span_two, _ = field.shape
    n = mix.shape[0]

    def kernel(c_ref, m_ref, *rest):
        outs = iter(rest)
        c = wide(c_ref)
        for d in range(n):
            total = dot(m_ref[d], c)
            for lo, hi in cuts:
                out = next(outs)
                for t in range(per):
                    out[t] = group(total[lo:hi], t).astype(out.dtype)

    def spec(span):
        return pl.BlockSpec((per, span, LANES), lambda t: (t, 0, 0))

    outs = [
        jax.ShapeDtypeStruct((tiles, hi - lo, LANES), BF16 if d else F32)
        for d in range(n)
        for lo, hi in cuts
    ]
    found = pl.pallas_call(
        kernel,
        grid=(tiles // per,),
        in_specs=[spec(span_two), whole(mix.shape)],
        out_specs=[spec(o.shape[1]) for o in outs],
        out_shape=outs,
        compiler_params=params(),
        cost_estimate=cost(2 * field.size * n * span_two, outs),
        name="shares",
    )(field, mix)
    return [found[d * len(cuts) : (d + 1) * len(cuts)] for d in range(n)]


def add(left, right):
    return (left.astype(F32) + right.astype(F32)).astype(BF16)


def after(value, *others):
    return lax.optimization_barrier((value,) + others)[0]


def by_tiles(rows, cols, latent, cotangent, factor_one, factor_two):
    span_one, span_two, depth = latent.shape
    order_one, order_two = factor_one.shape[1], factor_two.shape[1]
    fold = LANES * rows // depth
    tiles = span_one // fold
    near = 4 * tiles // 7
    part = near // 2
    groups = [(0, part), (part, near), (near, tiles)]
    unit = -(-span_two // 32) * 16
    cuts = [(0, unit), (unit, span_two)]
    half = unit // 2
    per = rows
    place = lax.axis_index("col")
    swap = swap_matrix(fold)
    last = cols - 1

    def exchange(value):
        return lax.all_to_all(value, "row", split_axis=0, concat_axis=0, tiled=True)

    def flat(value):
        return value.reshape((-1,) + value.shape[2:])

    def turn(value):
        return jnp.transpose(value, (1, 0, 2))

    def move(value, pairs_of):
        return lax.ppermute(value, "col", pairs_of)

    def down(value, step):
        return move(value, [(c, c - 1) for c in range(1, cols + 1 - step)])

    def up(value, step):
        return move(value, [(c, c + 1) for c in range(step - 1, cols - 1)])

    padded = jnp.pad(factor_two, ((0, 0), (last * span_two, 0)))
    beside = lax.dynamic_slice(padded, (0, place * span_two), (span_two, cols * span_two))
    mix_far = beside.T.reshape(cols, span_two, span_two)[::-1]
    mix_near = jnp.stack(
        [mix_far[0]]
        + [move(mix_far[d], [(c, c - d) for c in range(d, cols)]) for d in range(1, cols)]
    )

    every = (0, span_two)
    first = flat(exchange(pack(cotangent, swap, groups[0], every, rows)))
    firsts = [first, down(first, 1)]
    far_part = pack(cotangent, swap, groups[2], every, rows)
    far_part = flat(exchange(after(far_part, first, mix_near)))
    for step in range(2, cols):
        firsts.append(down(firsts[-1], step))
    own = shares(far_part, mix_far, cuts, per)
    sums = []
    for q in range(len(cuts)):
        held = after(own[last][q], *sums)
        sums.append(move(held, [(c, c - 1) for c in range(last, cols)]))
    z_first = pack(latent, swap, (0, tiles), cuts[0], rows)
    block = cuts[0][1] * LANES
    extra = -(-factor_one.size // block)
    full_one = jnp.pad(factor_one.reshape(-1), (0, extra * block - factor_one.size))
    full_one = full_one.reshape(1, extra, cuts[0][1], LANES)
    full_one = jnp.broadcast_to(full_one, (rows,) + full_one.shape[1:])
    z_first = jnp.concatenate([z_first, full_one], axis=1)
    z_first = exchange(after(z_first, far_part, firsts[1]))
    full_one = z_first[:, tiles:].reshape(rows, -1)[:, : factor_one.size]
    z_first = z_first[:, :tiles]
    second = pack(cotangent, swap, groups[1], every, rows)
    second = flat(exchange(after(second, z_first, firsts[min(2, last)], sums[0])))

    full_one = full_one.reshape(order_one, order_one)
    spot = lax.broadcasted_iota(jnp.int32, (order_one, order_one), 0)
    target = lax.broadcasted_iota(jnp.int32, spot.shape, 1)
    unit_of, tile = spot // (rows * tiles), spot % (rows * tiles)
    pick_latent = (target == tile * fold + unit_of).astype(BF16)
    index = 0
    for lo, hi in groups:
        inside = (tile >= rows * lo) & (tile < rows * hi)
        here = tile - rows * lo
        here = here // (hi - lo) * span_one + (lo + here % (hi - lo)) * fold + unit_of
        index = jnp.where(inside, here, index)
    pick_cotan = (target == index).astype(BF16)
    left = dot_nt(dot(pick_cotan, full_one).astype(BF16), pick_latent).astype(BF16)
    left_t = left.T

    counts = [rows * (hi - lo) for lo, hi in groups]
    y_first, *v_first = raise_field(turn(flat(z_first)), left, fold, counts)
    v_first = [turn(v) for v in v_first]
    ups_first = [v_first[-1]]
    for step in range(1, cols):
        ups_first.append(up(ups_first[-1], step))
    seconds = [second, down(after(second, v_first[-1]), 1)]
    z_last = pack(latent, swap, (0, tiles), cuts[1], rows)

    def hop(q, back):
        value = sums[q] if back == last else add(sums[q], own[back][q])
        return move(value, [(c, c - 1) for c in range(back, cols)])

    later = max(last - 1, 0)
    if later:
        sums[0] = hop(0, later)
    z_last = exchange(after(z_last, second, firsts[last], sums[0]))
    z_last = after(z_last, seconds[1], sums[1])
    y_last, *v_last = raise_field(turn(flat(z_last)), left, fold, counts)
    v_last = [turn(v) for v in v_last]
    ups_last = [v_last[-1]]
    for step in range(1, cols):
        ups_last.append(up(ups_last[-1], step))
    for back in range(later - 1, 0, -1):
        sums[0] = hop(0, back)
    if later:
        sums[1] = hop(1, later)
    early = sums[1]
    for back in range(later - 1, 0, -1):
        sums[1] = hop(1, back)
    for step in range(2, cols):
        held = seconds[-1]
        if step == last:
            held = after(held, v_last[-1], ups_first[last], sums[0])
        seconds.append(down(held, step))
    bits = [(0, 0, half), (0, half, unit), (1, unit, span_two)]
    ends = [sums[q][:, lo - cuts[q][0] : hi - cuts[q][0]] for q, lo, hi in bits]

    w_near, grad_near = [], 0.0
    for g, chunk in enumerate((firsts, seconds)):
        held = [chunk[0]] + chunk[1:]
        if g:
            held[0] = after(held[0], early, ups_last[min(2, last)])
        else:
            held[0] = after(held[0], ups_last[1])
        *w, grad = gathered(held, [v_first[g], v_last[g]], mix_near, cuts, per)
        w_near.append(w)
        grad_near = grad_near + grad

    two, met, sent = [], [], []
    for d in range(cols):
        grad = pairs(far_part, [ups_first[d], ups_last[d]], per)
        met.append(grad)
        if d:
            grad = move(grad, [(c, c - d) for c in range(d, cols)])
            sent.append(grad)
        two.append(grad_near[d] + grad)
    two = jnp.concatenate(two, axis=0)
    two = jnp.pad(two, ((order_two - span_two, 0), (0, 0)))
    two = lax.dynamic_slice(
        two, (order_two - span_two - place * span_two, 0), (order_two, span_two)
    )
    two = two.reshape(rows, order_two // rows, span_two)

    grad_latent, one, moved, written = None, None, [], []
    for n, (q, lo, hi) in enumerate(bits):
        own_here = own[0][q][:, lo - cuts[q][0] : hi - cuts[q][0]]
        share = turn(add(ends[n], own_here))
        if n == 1:
            share = after(share, *met, sums[1], one)
        elif n == 2:
            share = after(share, *sent, one)
        parts = [turn(w[q][:, lo - cuts[q][0] : hi - cuts[q][0]]) for w in w_near] + [share]
        grad, w_y = finish(parts, left_t, fold)
        one = match(w_y, y_last if q else y_first, (lo - cuts[q][0]) // (2 * fold), one)
        grad = turn(grad).reshape(rows, tiles, hi - lo, LANES)
        moved = [exchange(after(grad, *moved, *written[:-1]))]
        where = (lo, hi, half if q == 0 else unit)
        grad_latent = unpack(moved[0], swap, latent.shape, where, grad_latent)
        written.append(grad_latent)

    one = dot(one.astype(BF16), pick_latent).astype(BF16)
    one = jnp.transpose(one.reshape(order_one, cols, order_one // cols), (1, 0, 2))
    total = lax.dynamic_index_in_dim(one, place, 0, keepdims=False).astype(F32)
    for d in range(1, cols):
        ring = [(c, (c + d) % cols) for c in range(cols)]
        mine = lax.dynamic_index_in_dim(one, (place + d) % cols, 0, keepdims=False)
        total = total + move(mine, ring).astype(F32)
    total = total.reshape(fold, rows * tiles, order_one // cols)
    total = jnp.concatenate(
        [
            total[:, rows * lo : rows * hi].reshape(fold, rows, hi - lo, order_one // cols)
            for lo, hi in groups
        ],
        axis=2,
    )
    total = jnp.transpose(total, (1, 2, 0, 3)).reshape(rows, span_one, order_one // cols)
    total = jnp.concatenate([total, two], axis=2)
    total = exchange(after(total, *moved, written[-2])).sum(0)
    grad_one = keep_lower(total[:, : order_one // cols], depth)
    grad_two = keep_lower(total[:, order_one // cols :], depth)
    return (grad_latent, grad_one, grad_two)


def tiles_fit(rows, cols, span_one, span_two, depth):
    if depth % LANES or depth % rows or LANES * rows % depth:
        return False
    fold = LANES * rows // depth
    if fold > LANES or LANES % fold or depth // LANES * fold != rows:
        return False
    return (
        cols > 1
        and rows % 8 == 0
        and span_one % fold == 0
        and span_one // fold >= 4
        and span_two % (2 * fold) == 0
        and span_two % 8 == 0
        and span_two >= 64
        and 16 % (2 * fold) == 0
    )


def solution(mesh):
    rows, cols = mesh.shape["row"], mesh.shape["col"]

    def on_device(latent, cotangent, factor_one, factor_two):
        if tiles_fit(rows, cols, *latent.shape):
            return by_tiles(rows, cols, latent, cotangent, factor_one, factor_two)
        return by_lines(latent, cotangent, factor_one, factor_two)

    placed = (P("row", "col", None), P("row", "col", None), P("row", None), P("col", None))
    return jax.shard_map(
        on_device,
        mesh=mesh,
        in_specs=placed,
        out_specs=(P("row", "col", None), P("row", "col"), P("row", "col")),
        check_vma=False,
    )
```

```python
import functools

import jax
import jax.numpy as jnp
from jax import lax
from jax.experimental import pallas as pl
from jax.experimental.pallas import tpu as pltpu
from jax.sharding import PartitionSpec as P

LANES = 128
F32, BF16 = jnp.float32, jnp.bfloat16


def contract_first(left, right):
    return lax.dot_general(
        left, right, (((0,), (0,)), ((), ())), preferred_element_type=F32
    )


def contract_last(left, right):
    return lax.dot_general(
        left, right, (((1,), (1,)), ((), ())), preferred_element_type=F32
    )


def keep_lower(portion, depth):
    span_rows, span_cols = portion.shape
    row_ids = lax.axis_index("row") * span_rows + lax.broadcasted_iota(
        jnp.int32, (span_rows, span_cols), 0
    )
    col_ids = lax.axis_index("col") * span_cols + lax.broadcasted_iota(
        jnp.int32, (span_rows, span_cols), 1
    )
    return jnp.where(row_ids >= col_ids, portion / depth, 0.0)


def reduce_grad(partial_value, depth):
    portion = lax.psum_scatter(partial_value, "row", scatter_dimension=0, tiled=True)
    portion = lax.psum_scatter(portion, "col", scatter_dimension=1, tiled=True)
    return keep_lower(portion, depth)


def by_lines(latent, cotangent, factor_one, factor_two):
    rows_one, rows_two, depth = latent.shape
    latent_flat = jnp.transpose(latent, (1, 0, 2)).reshape(rows_two, rows_one * depth)
    latent_two = lax.all_to_all(latent_flat, "col", split_axis=1, concat_axis=0, tiled=True)
    cotan_flat = cotangent.reshape(rows_one, rows_two * depth)
    cotan_one = lax.all_to_all(cotan_flat, "row", split_axis=1, concat_axis=0, tiled=True)
    full_one = lax.all_gather(factor_one, "row", axis=0, tiled=True)
    full_two = lax.all_gather(factor_two, "col", axis=0, tiled=True)
    mixed_two = jnp.dot(full_two, latent_two, preferred_element_type=F32)
    pulled_one = contract_first(full_one, cotan_one)
    mixed_two = mixed_two.astype(BF16)
    pulled_one = pulled_one.astype(BF16)
    mixed_back = lax.all_to_all(mixed_two, "col", split_axis=0, concat_axis=1, tiled=True)
    mixed_block = (
        mixed_back.reshape(rows_two, rows_one, depth)
        .transpose(1, 0, 2)
        .reshape(rows_one, rows_two * depth)
    )
    mixed_one = lax.all_to_all(mixed_block, "row", split_axis=1, concat_axis=0, tiled=True)
    pulled_back = lax.all_to_all(pulled_one, "row", split_axis=0, concat_axis=1, tiled=True)
    pulled_block = (
        pulled_back.reshape(rows_one, rows_two, depth)
        .transpose(1, 0, 2)
        .reshape(rows_two, rows_one * depth)
    )
    pulled_two = lax.all_to_all(pulled_block, "col", split_axis=1, concat_axis=0, tiled=True)
    grad_factor_one = reduce_grad(contract_last(cotan_one, mixed_one), depth)
    grad_factor_two = reduce_grad(contract_last(pulled_two, latent_two), depth)
    result_two = contract_first(full_two, pulled_two)
    result_two = result_two.astype(BF16)
    result_back = lax.all_to_all(result_two, "col", split_axis=0, concat_axis=1, tiled=True)
    grad_latent = result_back.reshape(rows_two, rows_one, depth).transpose(1, 0, 2)
    return (grad_latent, grad_factor_one, grad_factor_two)


def dot(left, right):
    return jnp.dot(left, right, preferred_element_type=F32)


def dot_nt(left, right):
    return lax.dot_general(
        left, right, (((1,), (1,)), ((), ())), preferred_element_type=F32
    )


def whole(shape):
    return pl.BlockSpec(shape, lambda *_: (0,) * len(shape))


def params():
    return pltpu.CompilerParams(vmem_limit_bytes=48 * 1024 * 1024)


def cost(flops, arrays):
    return pl.CostEstimate(flops=1, bytes_accessed=1, transcendentals=0)


def swap_matrix(fold):
    size = fold * LANES
    part = LANES // fold
    rows = lax.broadcasted_iota(jnp.int32, (size, size), 0)
    cols = lax.broadcasted_iota(jnp.int32, (size, size), 1)
    major, minor, lane = rows // LANES, (rows % LANES) // part, rows % part
    return (cols == minor * LANES + major * part + lane).astype(BF16)


def lanes_of(pieces):
    return jnp.concatenate(pieces, axis=-1)


def group(value, index):
    return value[:, index * LANES : (index + 1) * LANES]


HELD = pl.BlockSpec(memory_space=pl.ANY)


def pack(block, swap, tiles, span, rows):
    depth = block.shape[2]
    fold = swap.shape[0] // LANES
    first, count = tiles[0], tiles[1] - tiles[0]
    lo, hi = span
    wide_rows = hi - lo if lo % (hi - lo) == 0 else lo
    per = 3 if first % 3 == 0 and count % 3 == 0 else 1

    def kernel(x_ref, p_ref, o_ref):
        for t in range(per):
            for half in range(depth // LANES):
                at = half * LANES
                x = lanes_of([x_ref[t * fold + n, : hi - lo, at : at + LANES] for n in range(fold)])
                y = dot(x, p_ref[...]).astype(BF16)
                for n in range(fold):
                    o_ref[half * fold + n, t] = group(y, n)

    out = jax.ShapeDtypeStruct((rows, count, hi - lo, LANES), BF16)
    return pl.pallas_call(
        kernel,
        grid=(count // per,),
        in_specs=[
            pl.BlockSpec(
                (per * fold, wide_rows, depth), lambda t: (first // per + t, lo // wide_rows, 0)
            ),
            whole(swap.shape),
        ],
        out_specs=pl.BlockSpec((rows, per, hi - lo, LANES), lambda t: (0, t, 0, 0)),
        out_shape=out,
        compiler_params=params(),
        cost_estimate=cost(2 * out.size * swap.shape[0], (out, out)),
        name="pack",
    )(block, swap)


def unpack(part, swap, shape, where, before):
    rows, tiles, span, _ = part.shape
    fold = swap.shape[0] // LANES
    depth = shape[2]
    lo, hi, unit = where
    index = lo // unit
    extra = [] if before is None else [before]
    per = 3 if tiles % 3 == 0 else 1

    def kernel(x_ref, p_ref, *rest):
        o_ref = rest[-1]
        for t in range(per):
            for half in range(depth // LANES):
                x = lanes_of([x_ref[half * fold + n, t] for n in range(fold)])
                y = dot(x, p_ref[...]).astype(BF16)
                for n in range(fold):
                    at = half * LANES
                    o_ref[t * fold + n, :span, at : at + LANES] = group(y, n)

    return pl.pallas_call(
        kernel,
        grid=(tiles // per,),
        in_specs=[
            pl.BlockSpec((rows, per, span, LANES), lambda t: (0, t, 0, 0)),
            whole(swap.shape),
        ]
        + [HELD] * len(extra),
        out_specs=pl.BlockSpec((per * fold, unit, depth), lambda t: (t, index, 0)),
        out_shape=jax.ShapeDtypeStruct(shape, BF16),
        input_output_aliases={2: 0} if extra else {},
        compiler_params=params(),
        cost_estimate=cost(2 * part.size * swap.shape[0], (part, part)),
        name="unpack",
    )(part, swap, *extra)


def swapped(pieces):
    fold = len(pieces)
    width = LANES // fold
    return [
        lanes_of([x[:, n * width : (n + 1) * width] for x in pieces]) for n in range(fold)
    ]


def to_y(refs, base, fold):
    turned = [swapped([r[base + n].astype(F32) for n in range(fold)]) for r in refs]
    return jnp.concatenate([y[n] for n in range(fold) for y in turned], axis=0).astype(BF16)


def from_y(value, refs, base, fold):
    spans = [r.shape[1] for r in refs]
    total = sum(spans)
    start = 0
    for r, span in zip(refs, spans):
        y = swapped([value[n * total + start : n * total + start + span] for n in range(fold)])
        for n in range(fold):
            r[base + n] = y[n].astype(BF16)
        start += span


def raise_field(field, left, fold, spans):
    span_two = field.shape[0]
    order = left.shape[0]
    step = 2 * fold
    count = span_two // step

    def kernel(x_ref, l_ref, y_ref, *outs):
        y = lanes_of([to_y([x_ref], u * fold, fold) for u in range(2)])
        y_ref[0] = y
        v = dot(l_ref[...], y)
        for u in range(2):
            from_y(group(v, u), outs, u * fold, fold)

    shapes = [jax.ShapeDtypeStruct((span_two, span, LANES), BF16) for span in spans]
    y_shape = jax.ShapeDtypeStruct((count, order, 2 * LANES), BF16)
    return pl.pallas_call(
        kernel,
        grid=(count,),
        in_specs=[pl.BlockSpec((step,) + field.shape[1:], lambda t: (t, 0, 0)), whole(left.shape)],
        out_specs=[pl.BlockSpec((1, order, 2 * LANES), lambda t: (t, 0, 0))]
        + [pl.BlockSpec((step, span, LANES), lambda t: (t, 0, 0)) for span in spans],
        out_shape=[y_shape] + shapes,
        compiler_params=params(),
        cost_estimate=cost(2 * y_shape.size * order, (y_shape,) * 3),
        name="raise_field",
    )(field, left)


def finish(parts, left_t, fold):
    span_two = parts[0].shape[0]
    order = left_t.shape[0]
    step = 2 * fold
    count = span_two // step
    n = len(parts)

    def kernel(*refs):
        ins, l_ref, out_ref, y_ref = refs[:n], refs[n], refs[n + 1], refs[n + 2]
        w = lanes_of([to_y(ins, u * fold, fold) for u in range(2)])
        y_ref[0] = w
        v = dot(l_ref[...], w)
        for u in range(2):
            from_y(group(v, u), [out_ref], u * fold, fold)

    out = jax.ShapeDtypeStruct((span_two, order // fold, LANES), BF16)
    y_shape = jax.ShapeDtypeStruct((count, order, 2 * LANES), BF16)
    return pl.pallas_call(
        kernel,
        grid=(count,),
        in_specs=[pl.BlockSpec((step,) + p.shape[1:], lambda t: (t, 0, 0)) for p in parts]
        + [whole(left_t.shape)],
        out_specs=[
            pl.BlockSpec((step,) + out.shape[1:], lambda t: (t, 0, 0)),
            pl.BlockSpec((1, order, 2 * LANES), lambda t: (t, 0, 0)),
        ],
        out_shape=[out, y_shape],
        compiler_params=params(),
        cost_estimate=cost(2 * out.size * order, (out,) * 3),
        name="finish",
    )(*parts, left_t)


def match(w, z, first, before):
    count, order, width = w.shape
    extra = [] if before is None else [before]

    def kernel(w_ref, z_ref, *rest):
        g_ref = rest[-1]

        @pl.when(pl.program_id(0) == 0)
        def _():
            g_ref[...] = jnp.zeros_like(g_ref) if before is None else rest[0][...]

        g_ref[...] += dot_nt(w_ref[0], z_ref[0])

    g_shape = jax.ShapeDtypeStruct((order, order), F32)
    return pl.pallas_call(
        kernel,
        grid=(count,),
        in_specs=[
            pl.BlockSpec((1, order, width), lambda t: (t, 0, 0)),
            pl.BlockSpec((1, order, width), lambda t: (first + t, 0, 0)),
        ]
        + [whole(b.shape) for b in extra],
        out_specs=whole(g_shape.shape),
        out_shape=g_shape,
        compiler_params=params(),
        cost_estimate=cost(2 * w.size * order, (w, w)),
        name="match",
    )(w, z, *extra)


def wide(ref):
    return lanes_of([ref[t] for t in range(ref.shape[0])])


def tall(refs):
    return jnp.concatenate([wide(r) for r in refs], axis=0)


def gathered(slots, fields, mix, cuts, per):
    tiles, span_two, _ = slots[0].shape
    n, m = len(slots), len(fields)

    def kernel(*refs):
        ins, vs, m_ref = refs[:n], refs[n : n + m], refs[n + m]
        outs, g_ref = refs[n + m + 1 : -1], refs[-1]

        @pl.when(pl.program_id(0) == 0)
        def _():
            g_ref[...] = jnp.zeros_like(g_ref)

        v = tall(vs)
        total = None
        for d in range(n):
            c = wide(ins[d])
            g_ref[d] += dot_nt(c, v)
            term = dot(m_ref[d], c)
            total = term if total is None else total + term
        total = total.astype(BF16)
        for (lo, hi), out in zip(cuts, outs):
            for t in range(per):
                out[t] = group(total[lo:hi], t)

    def spec(span):
        return pl.BlockSpec((per, span, LANES), lambda t: (t, 0, 0))

    g_shape = jax.ShapeDtypeStruct((n, span_two, span_two), F32)
    return pl.pallas_call(
        kernel,
        grid=(tiles // per,),
        in_specs=[spec(span_two)] * n + [spec(f.shape[1]) for f in fields] + [whole(mix.shape)],
        out_specs=[spec(hi - lo) for lo, hi in cuts] + [whole(g_shape.shape)],
        out_shape=[jax.ShapeDtypeStruct((tiles, hi - lo, LANES), BF16) for lo, hi in cuts]
        + [g_shape],
        compiler_params=params(),
        cost_estimate=cost(4 * slots[0].size * n * span_two, tuple(slots) + tuple(slots[:2])),
        name="gathered",
    )(*slots, *fields, mix)


def pairs(field, others, per):
    tiles, span_two, _ = field.shape
    n = len(others)

    def kernel(*refs):
        c_ref, ins, g_ref = refs[0], refs[1 : n + 1], refs[-1]

        @pl.when(pl.program_id(0) == 0)
        def _():
            g_ref[...] = jnp.zeros_like(g_ref)

        g_ref[...] += dot_nt(wide(c_ref), tall(ins))

    def spec(span):
        return pl.BlockSpec((per, span, LANES), lambda t: (t, 0, 0))

    g_shape = jax.ShapeDtypeStruct((span_two, span_two), F32)
    return pl.pallas_call(
        kernel,
        grid=(tiles // per,),
        in_specs=[spec(span_two)] + [spec(o.shape[1]) for o in others],
        out_specs=whole(g_shape.shape),
        out_shape=g_shape,
        compiler_params=params(),
        cost_estimate=cost(2 * field.size * span_two, (field, field)),
        name="pairs",
    )(field, *others)


def shares(field, mix, cuts, per):
    tiles, span_two, _ = field.shape
    n = mix.shape[0]

    def kernel(c_ref, m_ref, *rest):
        outs = iter(rest)
        c = wide(c_ref)
        for d in range(n):
            total = dot(m_ref[d], c)
            for lo, hi in cuts:
                out = next(outs)
                for t in range(per):
                    out[t] = group(total[lo:hi], t).astype(out.dtype)

    def spec(span):
        return pl.BlockSpec((per, span, LANES), lambda t: (t, 0, 0))

    outs = [
        jax.ShapeDtypeStruct((tiles, hi - lo, LANES), BF16 if d else F32)
        for d in range(n)
        for lo, hi in cuts
    ]
    found = pl.pallas_call(
        kernel,
        grid=(tiles // per,),
        in_specs=[spec(span_two), whole(mix.shape)],
        out_specs=[spec(o.shape[1]) for o in outs],
        out_shape=outs,
        compiler_params=params(),
        cost_estimate=cost(2 * field.size * n * span_two, outs),
        name="shares",
    )(field, mix)
    return [found[d * len(cuts) : (d + 1) * len(cuts)] for d in range(n)]


def add(left, right):
    return (left.astype(F32) + right.astype(F32)).astype(BF16)


def after(value, *others):
    return lax.optimization_barrier((value,) + others)[0]


def by_tiles(rows, cols, latent, cotangent, factor_one, factor_two):
    span_one, span_two, depth = latent.shape
    order_one, order_two = factor_one.shape[1], factor_two.shape[1]
    fold = LANES * rows // depth
    tiles = span_one // fold
    near = 4 * tiles // 7
    part = near // 2
    groups = [(0, part), (part, near), (near, tiles)]
    unit = -(-span_two // 32) * 16
    cuts = [(0, unit), (unit, span_two)]
    half = unit // 2
    per = rows
    place = lax.axis_index("col")
    swap = swap_matrix(fold)
    last = cols - 1

    def exchange(value):
        return lax.all_to_all(value, "row", split_axis=0, concat_axis=0, tiled=True)

    def flat(value):
        return value.reshape((-1,) + value.shape[2:])

    def turn(value):
        return jnp.transpose(value, (1, 0, 2))

    def move(value, pairs_of):
        return lax.ppermute(value, "col", pairs_of)

    def down(value, step):
        return move(value, [(c, c - 1) for c in range(1, cols + 1 - step)])

    def up(value, step):
        return move(value, [(c, c + 1) for c in range(step - 1, cols - 1)])

    padded = jnp.pad(factor_two, ((0, 0), (last * span_two, 0)))
    beside = lax.dynamic_slice(padded, (0, place * span_two), (span_two, cols * span_two))
    mix_far = beside.T.reshape(cols, span_two, span_two)[::-1]
    mix_near = jnp.stack(
        [mix_far[0]]
        + [move(mix_far[d], [(c, c - d) for c in range(d, cols)]) for d in range(1, cols)]
    )

    every = (0, span_two)
    first = flat(exchange(pack(cotangent, swap, groups[0], every, rows)))
    firsts = [first, down(first, 1)]
    far_part = pack(cotangent, swap, groups[2], every, rows)
    far_part = flat(exchange(after(far_part, first, mix_near)))
    for step in range(2, cols):
        firsts.append(down(firsts[-1], step))
    own = shares(far_part, mix_far, cuts, per)
    sums = []
    for q in range(len(cuts)):
        held = after(own[last][q], *sums)
        sums.append(move(held, [(c, c - 1) for c in range(last, cols)]))
    z_first = pack(latent, swap, (0, tiles), cuts[0], rows)
    block = cuts[0][1] * LANES
    extra = -(-factor_one.size // block)
    full_one = jnp.pad(factor_one.reshape(-1), (0, extra * block - factor_one.size))
    full_one = full_one.reshape(1, extra, cuts[0][1], LANES)
    full_one = jnp.broadcast_to(full_one, (rows,) + full_one.shape[1:])
    z_first = jnp.concatenate([z_first, full_one], axis=1)
    z_first = exchange(after(z_first, far_part, firsts[1]))
    full_one = z_first[:, tiles:].reshape(rows, -1)[:, : factor_one.size]
    z_first = z_first[:, :tiles]
    second = pack(cotangent, swap, groups[1], every, rows)
    second = flat(exchange(after(second, z_first, firsts[min(2, last)], sums[0])))

    full_one = full_one.reshape(order_one, order_one)
    spot = lax.broadcasted_iota(jnp.int32, (order_one, order_one), 0)
    target = lax.broadcasted_iota(jnp.int32, spot.shape, 1)
    unit_of, tile = spot // (rows * tiles), spot % (rows * tiles)
    pick_latent = (target == tile * fold + unit_of).astype(BF16)
    index = 0
    for lo, hi in groups:
        inside = (tile >= rows * lo) & (tile < rows * hi)
        here = tile - rows * lo
        here = here // (hi - lo) * span_one + (lo + here % (hi - lo)) * fold + unit_of
        index = jnp.where(inside, here, index)
    pick_cotan = (target == index).astype(BF16)
    left = dot_nt(dot(pick_cotan, full_one).astype(BF16), pick_latent).astype(BF16)
    left_t = left.T

    counts = [rows * (hi - lo) for lo, hi in groups]
    y_first, *v_first = raise_field(turn(flat(z_first)), left, fold, counts)
    v_first = [turn(v) for v in v_first]
    ups_first = [v_first[-1]]
    for step in range(1, cols):
        ups_first.append(up(ups_first[-1], step))
    seconds = [second, down(after(second, v_first[-1]), 1)]
    z_last = pack(latent, swap, (0, tiles), cuts[1], rows)

    def hop(q, back):
        value = sums[q] if back == last else add(sums[q], own[back][q])
        return move(value, [(c, c - 1) for c in range(back, cols)])

    later = max(last - 1, 0)
    if later:
        sums[0] = hop(0, later)
    z_last = exchange(after(z_last, second, firsts[last], sums[0]))
    z_last = after(z_last, seconds[1], sums[1])
    y_last, *v_last = raise_field(turn(flat(z_last)), left, fold, counts)
    v_last = [turn(v) for v in v_last]
    ups_last = [v_last[-1]]
    for step in range(1, cols):
        ups_last.append(up(ups_last[-1], step))
    for back in range(later - 1, 1, -1):
        sums[0] = hop(0, back)
    if later:
        sums[1] = hop(1, later)
    early = sums[1]
    for back in range(later - 1, 1, -1):
        sums[1] = hop(1, back)
    for step in range(2, cols):
        held = seconds[-1]
        if step == last:
            held = after(held, v_last[-1], ups_first[1])
        seconds.append(down(held, step))

    bits = [(0, 0, half), (0, half, unit), (1, unit, span_two)]
    ends = []
    if later > 1:
        sums = [add(sums[q], own[1][q]) for q in range(2)]
    for q, lo, hi in bits:
        held = sums[q][:, lo - cuts[q][0] : hi - cuts[q][0]]
        if later > 1:
            held = after(held, ends[0] if ends else seconds[-2])
            held = move(held, [(c, c - 1) for c in range(1, cols)])
        ends.append(held)

    def second_factor(met, sent, grad_near):
        two = [grad_near[d] + (sent[d - 1] if d else met[0]) for d in range(cols)]
        two = jnp.concatenate(two, axis=0)
        two = jnp.pad(two, ((order_two - span_two, 0), (0, 0)))
        two = lax.dynamic_slice(
            two, (order_two - span_two - place * span_two, 0), (order_two, span_two)
        )
        return two.reshape(rows, order_two // rows, span_two)

    met = [pairs(far_part, [ups_first[d], ups_last[d]], per) for d in range(cols)]
    sent = [move(met[d], [(c, c - d) for c in range(d, cols)]) for d in range(1, cols)]

    w_near, grad_near = [], 0.0
    for g, chunk in enumerate((firsts, seconds)):
        held = [chunk[0]] + chunk[1:]
        if g:
            held[0] = after(held[0], early, met[min(2, last)], ups_first[last])
        else:
            held[0] = after(held[0], met[0], met[1])
        *w, grad = gathered(held, [v_first[g], v_last[g]], mix_near, cuts, per)
        w_near.append(w)
        grad_near = grad_near + grad
    one, moved = None, []
    for n, (q, lo, hi) in enumerate(bits):
        own_here = own[0][q][:, lo - cuts[q][0] : hi - cuts[q][0]]
        share = turn(add(ends[n], own_here))
        if n == 0:
            share = after(share, ends[2])
        else:
            share = after(share, one, *sent[:2])
        parts = [turn(w[q][:, lo - cuts[q][0] : hi - cuts[q][0]]) for w in w_near] + [share]
        grad, w_y = finish(parts, left_t, fold)
        one = match(w_y, y_last if q else y_first, (lo - cuts[q][0]) // (2 * fold), one)
        grad = turn(grad).reshape(rows, tiles, hi - lo, LANES)
        moved.append(exchange(after(grad, *moved[-1:])))

    one = dot(one.astype(BF16), pick_latent).astype(BF16)
    one = one.reshape(fold, rows * tiles, order_one)
    one = jnp.concatenate(
        [
            one[:, rows * lo : rows * hi].reshape(fold, rows, hi - lo, order_one)
            for lo, hi in groups
        ],
        axis=2,
    )
    one = jnp.transpose(one, (1, 2, 0, 3)).reshape(rows, span_one, order_one)
    where = [(lo, hi, half if q == 0 else unit) for q, lo, hi in bits]
    grad_latent = unpack(moved[0], swap, latent.shape, where[0], None)
    grad_latent = unpack(moved[1], swap, latent.shape, where[1], grad_latent)
    one, grad_latent = lax.optimization_barrier((one, grad_latent))
    one = exchange(after(one, moved[2], ups_last[last]))
    grad_latent = unpack(moved[2], swap, latent.shape, where[2], grad_latent)
    one = one.astype(F32).sum(0)
    one = jnp.transpose(one.reshape(span_one, cols, order_one // cols), (1, 0, 2))
    total = lax.dynamic_index_in_dim(one, place, 0, keepdims=False)
    for d in range(1, cols):
        ring = [(c, (c + d) % cols) for c in range(cols)]
        mine = lax.dynamic_index_in_dim(one, (place + d) % cols, 0, keepdims=False)
        total = total + move(mine, ring)
    grad_one = keep_lower(total, depth)
    sent[-1], grad_latent = lax.optimization_barrier((sent[-1], grad_latent))
    two = second_factor(met, sent, grad_near)
    two = exchange(after(two, one)).sum(0)
    grad_two = keep_lower(two, depth)
    return (grad_latent, grad_one, grad_two)


def tiles_fit(rows, cols, span_one, span_two, depth):
    if depth % LANES or depth % rows or LANES * rows % depth:
        return False
    fold = LANES * rows // depth
    if fold > LANES or LANES % fold or depth // LANES * fold != rows:
        return False
    return (
        cols > 1
        and rows % 8 == 0
        and span_one % fold == 0
        and span_one // fold >= 4
        and span_two % (2 * fold) == 0
        and span_two % 8 == 0
        and span_two >= 64
        and 16 % (2 * fold) == 0
    )


def solution(mesh):
    rows, cols = mesh.shape["row"], mesh.shape["col"]

    def on_device(latent, cotangent, factor_one, factor_two):
        if tiles_fit(rows, cols, *latent.shape):
            return by_tiles(rows, cols, latent, cotangent, factor_one, factor_two)
        return by_lines(latent, cotangent, factor_one, factor_two)

    placed = (P("row", "col", None), P("row", "col", None), P("row", None), P("col", None))
    return jax.shard_map(
        on_device,
        mesh=mesh,
        in_specs=placed,
        out_specs=(P("row", "col", None), P("row", "col"), P("row", "col")),
        check_vma=False,
    )
```

```python
import functools

import jax
import jax.numpy as jnp
from jax import lax
from jax.experimental import pallas as pl
from jax.experimental.pallas import tpu as pltpu
from jax.sharding import PartitionSpec as P

LANES = 128
F32, BF16 = jnp.float32, jnp.bfloat16


def contract_first(left, right):
    return lax.dot_general(
        left, right, (((0,), (0,)), ((), ())), preferred_element_type=F32
    )


def contract_last(left, right):
    return lax.dot_general(
        left, right, (((1,), (1,)), ((), ())), preferred_element_type=F32
    )


def keep_lower(portion, depth):
    span_rows, span_cols = portion.shape
    row_ids = lax.axis_index("row") * span_rows + lax.broadcasted_iota(
        jnp.int32, (span_rows, span_cols), 0
    )
    col_ids = lax.axis_index("col") * span_cols + lax.broadcasted_iota(
        jnp.int32, (span_rows, span_cols), 1
    )
    return jnp.where(row_ids >= col_ids, portion / depth, 0.0)


def reduce_grad(partial_value, depth):
    portion = lax.psum_scatter(partial_value, "row", scatter_dimension=0, tiled=True)
    portion = lax.psum_scatter(portion, "col", scatter_dimension=1, tiled=True)
    return keep_lower(portion, depth)


def by_lines(latent, cotangent, factor_one, factor_two):
    rows_one, rows_two, depth = latent.shape
    latent_flat = jnp.transpose(latent, (1, 0, 2)).reshape(rows_two, rows_one * depth)
    latent_two = lax.all_to_all(latent_flat, "col", split_axis=1, concat_axis=0, tiled=True)
    cotan_flat = cotangent.reshape(rows_one, rows_two * depth)
    cotan_one = lax.all_to_all(cotan_flat, "row", split_axis=1, concat_axis=0, tiled=True)
    full_one = lax.all_gather(factor_one, "row", axis=0, tiled=True)
    full_two = lax.all_gather(factor_two, "col", axis=0, tiled=True)
    mixed_two = jnp.dot(full_two, latent_two, preferred_element_type=F32)
    pulled_one = contract_first(full_one, cotan_one)
    mixed_two = mixed_two.astype(BF16)
    pulled_one = pulled_one.astype(BF16)
    mixed_back = lax.all_to_all(mixed_two, "col", split_axis=0, concat_axis=1, tiled=True)
    mixed_block = (
        mixed_back.reshape(rows_two, rows_one, depth)
        .transpose(1, 0, 2)
        .reshape(rows_one, rows_two * depth)
    )
    mixed_one = lax.all_to_all(mixed_block, "row", split_axis=1, concat_axis=0, tiled=True)
    pulled_back = lax.all_to_all(pulled_one, "row", split_axis=0, concat_axis=1, tiled=True)
    pulled_block = (
        pulled_back.reshape(rows_one, rows_two, depth)
        .transpose(1, 0, 2)
        .reshape(rows_two, rows_one * depth)
    )
    pulled_two = lax.all_to_all(pulled_block, "col", split_axis=1, concat_axis=0, tiled=True)
    grad_factor_one = reduce_grad(contract_last(cotan_one, mixed_one), depth)
    grad_factor_two = reduce_grad(contract_last(pulled_two, latent_two), depth)
    result_two = contract_first(full_two, pulled_two)
    result_two = result_two.astype(BF16)
    result_back = lax.all_to_all(result_two, "col", split_axis=0, concat_axis=1, tiled=True)
    grad_latent = result_back.reshape(rows_two, rows_one, depth).transpose(1, 0, 2)
    return (grad_latent, grad_factor_one, grad_factor_two)


def dot(left, right):
    return jnp.dot(left, right, preferred_element_type=F32)


def dot_nt(left, right):
    return lax.dot_general(
        left, right, (((1,), (1,)), ((), ())), preferred_element_type=F32
    )


def whole(shape):
    return pl.BlockSpec(shape, lambda *_: (0,) * len(shape))


def params():
    return pltpu.CompilerParams(vmem_limit_bytes=48 * 1024 * 1024)


def cost(flops, arrays):
    return pl.CostEstimate(flops=1, bytes_accessed=1, transcendentals=0)


def swap_matrix(fold):
    size = fold * LANES
    part = LANES // fold
    rows = lax.broadcasted_iota(jnp.int32, (size, size), 0)
    cols = lax.broadcasted_iota(jnp.int32, (size, size), 1)
    major, minor, lane = rows // LANES, (rows % LANES) // part, rows % part
    return (cols == minor * LANES + major * part + lane).astype(BF16)


def lanes_of(pieces):
    return jnp.concatenate(pieces, axis=-1)


def group(value, index):
    return value[:, index * LANES : (index + 1) * LANES]


HELD = pl.BlockSpec(memory_space=pl.ANY)


def pack(block, swap, tiles, span, rows):
    depth = block.shape[2]
    fold = swap.shape[0] // LANES
    first, count = tiles[0], tiles[1] - tiles[0]
    lo, hi = span
    wide_rows = hi - lo if lo % (hi - lo) == 0 else lo
    per = 3 if first % 3 == 0 and count % 3 == 0 else 1

    def kernel(x_ref, p_ref, o_ref):
        for t in range(per):
            for half in range(depth // LANES):
                at = half * LANES
                x = lanes_of([x_ref[t * fold + n, : hi - lo, at : at + LANES] for n in range(fold)])
                y = dot(x, p_ref[...]).astype(BF16)
                for n in range(fold):
                    o_ref[half * fold + n, t] = group(y, n)

    out = jax.ShapeDtypeStruct((rows, count, hi - lo, LANES), BF16)
    return pl.pallas_call(
        kernel,
        grid=(count // per,),
        in_specs=[
            pl.BlockSpec(
                (per * fold, wide_rows, depth), lambda t: (first // per + t, lo // wide_rows, 0)
            ),
            whole(swap.shape),
        ],
        out_specs=pl.BlockSpec((rows, per, hi - lo, LANES), lambda t: (0, t, 0, 0)),
        out_shape=out,
        compiler_params=params(),
        cost_estimate=cost(2 * out.size * swap.shape[0], (out, out)),
        name="pack",
    )(block, swap)


def unpack(part, swap, shape, where, before):
    rows, tiles, span, _ = part.shape
    fold = swap.shape[0] // LANES
    depth = shape[2]
    lo, hi, unit = where
    index = lo // unit
    extra = [] if before is None else [before]
    per = 3 if tiles % 3 == 0 else 1

    def kernel(x_ref, p_ref, *rest):
        o_ref = rest[-1]
        for t in range(per):
            for half in range(depth // LANES):
                x = lanes_of([x_ref[half * fold + n, t] for n in range(fold)])
                y = dot(x, p_ref[...]).astype(BF16)
                for n in range(fold):
                    at = half * LANES
                    o_ref[t * fold + n, :span, at : at + LANES] = group(y, n)

    return pl.pallas_call(
        kernel,
        grid=(tiles // per,),
        in_specs=[
            pl.BlockSpec((rows, per, span, LANES), lambda t: (0, t, 0, 0)),
            whole(swap.shape),
        ]
        + [HELD] * len(extra),
        out_specs=pl.BlockSpec((per * fold, unit, depth), lambda t: (t, index, 0)),
        out_shape=jax.ShapeDtypeStruct(shape, BF16),
        input_output_aliases={2: 0} if extra else {},
        compiler_params=params(),
        cost_estimate=cost(2 * part.size * swap.shape[0], (part, part)),
        name="unpack",
    )(part, swap, *extra)


def swapped(pieces):
    fold = len(pieces)
    width = LANES // fold
    return [
        lanes_of([x[:, n * width : (n + 1) * width] for x in pieces]) for n in range(fold)
    ]


def to_y(refs, base, fold):
    turned = [swapped([r[base + n].astype(F32) for n in range(fold)]) for r in refs]
    return jnp.concatenate([y[n] for n in range(fold) for y in turned], axis=0).astype(BF16)


def from_y(value, refs, base, fold):
    spans = [r.shape[1] for r in refs]
    total = sum(spans)
    start = 0
    for r, span in zip(refs, spans):
        y = swapped([value[n * total + start : n * total + start + span] for n in range(fold)])
        for n in range(fold):
            r[base + n] = y[n].astype(BF16)
        start += span


def raise_field(field, left, fold, spans):
    span_two = field.shape[0]
    order = left.shape[0]
    step = 2 * fold
    count = span_two // step

    def kernel(x_ref, l_ref, y_ref, *outs):
        y = lanes_of([to_y([x_ref], u * fold, fold) for u in range(2)])
        y_ref[0] = y
        v = dot(l_ref[...], y)
        for u in range(2):
            from_y(group(v, u), outs, u * fold, fold)

    shapes = [jax.ShapeDtypeStruct((span_two, span, LANES), BF16) for span in spans]
    y_shape = jax.ShapeDtypeStruct((count, order, 2 * LANES), BF16)
    return pl.pallas_call(
        kernel,
        grid=(count,),
        in_specs=[pl.BlockSpec((step,) + field.shape[1:], lambda t: (t, 0, 0)), whole(left.shape)],
        out_specs=[pl.BlockSpec((1, order, 2 * LANES), lambda t: (t, 0, 0))]
        + [pl.BlockSpec((step, span, LANES), lambda t: (t, 0, 0)) for span in spans],
        out_shape=[y_shape] + shapes,
        compiler_params=params(),
        cost_estimate=cost(2 * y_shape.size * order, (y_shape,) * 3),
        name="raise_field",
    )(field, left)


def finish(parts, left_t, fold):
    span_two = parts[0].shape[0]
    order = left_t.shape[0]
    step = 2 * fold
    count = span_two // step
    n = len(parts)

    def kernel(*refs):
        ins, l_ref, out_ref, y_ref = refs[:n], refs[n], refs[n + 1], refs[n + 2]
        w = lanes_of([to_y(ins, u * fold, fold) for u in range(2)])
        y_ref[0] = w
        v = dot(l_ref[...], w)
        for u in range(2):
            from_y(group(v, u), [out_ref], u * fold, fold)

    out = jax.ShapeDtypeStruct((span_two, order // fold, LANES), BF16)
    y_shape = jax.ShapeDtypeStruct((count, order, 2 * LANES), BF16)
    return pl.pallas_call(
        kernel,
        grid=(count,),
        in_specs=[pl.BlockSpec((step,) + p.shape[1:], lambda t: (t, 0, 0)) for p in parts]
        + [whole(left_t.shape)],
        out_specs=[
            pl.BlockSpec((step,) + out.shape[1:], lambda t: (t, 0, 0)),
            pl.BlockSpec((1, order, 2 * LANES), lambda t: (t, 0, 0)),
        ],
        out_shape=[out, y_shape],
        compiler_params=params(),
        cost_estimate=cost(2 * out.size * order, (out,) * 3),
        name="finish",
    )(*parts, left_t)


def match(w, z, first, before):
    count, order, width = w.shape
    extra = [] if before is None else [before]

    def kernel(w_ref, z_ref, *rest):
        g_ref = rest[-1]

        @pl.when(pl.program_id(0) == 0)
        def _():
            g_ref[...] = jnp.zeros_like(g_ref) if before is None else rest[0][...]

        g_ref[...] += dot_nt(w_ref[0], z_ref[0])

    g_shape = jax.ShapeDtypeStruct((order, order), F32)
    return pl.pallas_call(
        kernel,
        grid=(count,),
        in_specs=[
            pl.BlockSpec((1, order, width), lambda t: (t, 0, 0)),
            pl.BlockSpec((1, order, width), lambda t: (first + t, 0, 0)),
        ]
        + [whole(b.shape) for b in extra],
        out_specs=whole(g_shape.shape),
        out_shape=g_shape,
        compiler_params=params(),
        cost_estimate=cost(2 * w.size * order, (w, w)),
        name="match",
    )(w, z, *extra)


def wide(ref):
    return lanes_of([ref[t] for t in range(ref.shape[0])])


def tall(refs):
    return jnp.concatenate([wide(r) for r in refs], axis=0)


def gathered(slots, fields, mix, cuts, per):
    tiles, span_two, _ = slots[0].shape
    n, m = len(slots), len(fields)

    def kernel(*refs):
        ins, vs, m_ref = refs[:n], refs[n : n + m], refs[n + m]
        outs, g_ref = refs[n + m + 1 : -1], refs[-1]

        @pl.when(pl.program_id(0) == 0)
        def _():
            g_ref[...] = jnp.zeros_like(g_ref)

        v = tall(vs)
        total = None
        for d in range(n):
            c = wide(ins[d])
            g_ref[d] += dot_nt(c, v)
            term = dot(m_ref[d], c)
            total = term if total is None else total + term
        total = total.astype(BF16)
        for (lo, hi), out in zip(cuts, outs):
            for t in range(per):
                out[t] = group(total[lo:hi], t)

    def spec(span):
        return pl.BlockSpec((per, span, LANES), lambda t: (t, 0, 0))

    g_shape = jax.ShapeDtypeStruct((n, span_two, span_two), F32)
    return pl.pallas_call(
        kernel,
        grid=(tiles // per,),
        in_specs=[spec(span_two)] * n + [spec(f.shape[1]) for f in fields] + [whole(mix.shape)],
        out_specs=[spec(hi - lo) for lo, hi in cuts] + [whole(g_shape.shape)],
        out_shape=[jax.ShapeDtypeStruct((tiles, hi - lo, LANES), BF16) for lo, hi in cuts]
        + [g_shape],
        compiler_params=params(),
        cost_estimate=cost(4 * slots[0].size * n * span_two, tuple(slots) + tuple(slots[:2])),
        name="gathered",
    )(*slots, *fields, mix)


def pairs(field, others, per):
    tiles, span_two, _ = field.shape
    n = len(others)

    def kernel(*refs):
        c_ref, ins, g_ref = refs[0], refs[1 : n + 1], refs[-1]

        @pl.when(pl.program_id(0) == 0)
        def _():
            g_ref[...] = jnp.zeros_like(g_ref)

        g_ref[...] += dot_nt(wide(c_ref), tall(ins))

    def spec(span):
        return pl.BlockSpec((per, span, LANES), lambda t: (t, 0, 0))

    g_shape = jax.ShapeDtypeStruct((span_two, span_two), F32)
    return pl.pallas_call(
        kernel,
        grid=(tiles // per,),
        in_specs=[spec(span_two)] + [spec(o.shape[1]) for o in others],
        out_specs=whole(g_shape.shape),
        out_shape=g_shape,
        compiler_params=params(),
        cost_estimate=cost(2 * field.size * span_two, (field, field)),
        name="pairs",
    )(field, *others)


def shares(field, mix, cuts, per):
    tiles, span_two, _ = field.shape
    n = mix.shape[0]

    def kernel(c_ref, m_ref, *rest):
        outs = iter(rest)
        c = wide(c_ref)
        for d in range(n):
            total = dot(m_ref[d], c)
            for lo, hi in cuts:
                out = next(outs)
                for t in range(per):
                    out[t] = group(total[lo:hi], t).astype(out.dtype)

    def spec(span):
        return pl.BlockSpec((per, span, LANES), lambda t: (t, 0, 0))

    outs = [
        jax.ShapeDtypeStruct((tiles, hi - lo, LANES), BF16 if d else F32)
        for d in range(n)
        for lo, hi in cuts
    ]
    found = pl.pallas_call(
        kernel,
        grid=(tiles // per,),
        in_specs=[spec(span_two), whole(mix.shape)],
        out_specs=[spec(o.shape[1]) for o in outs],
        out_shape=outs,
        compiler_params=params(),
        cost_estimate=cost(2 * field.size * n * span_two, outs),
        name="shares",
    )(field, mix)
    return [found[d * len(cuts) : (d + 1) * len(cuts)] for d in range(n)]


def add(left, right):
    return (left.astype(F32) + right.astype(F32)).astype(BF16)


def after(value, *others):
    return lax.optimization_barrier((value,) + others)[0]


def by_tiles(rows, cols, latent, cotangent, factor_one, factor_two):
    span_one, span_two, depth = latent.shape
    order_one, order_two = factor_one.shape[1], factor_two.shape[1]
    fold = LANES * rows // depth
    tiles = span_one // fold
    near = 4 * tiles // 7
    part = near // 2
    groups = [(0, part), (part, near), (near, tiles)]
    unit = -(-span_two // 32) * 16
    cuts = [(0, unit), (unit, span_two)]
    half = unit // 2
    per = rows
    place = lax.axis_index("col")
    swap = swap_matrix(fold)
    last = cols - 1

    def exchange(value):
        return lax.all_to_all(value, "row", split_axis=0, concat_axis=0, tiled=True)

    def flat(value):
        return value.reshape((-1,) + value.shape[2:])

    def turn(value):
        return jnp.transpose(value, (1, 0, 2))

    def move(value, pairs_of):
        return lax.ppermute(value, "col", pairs_of)

    def down(value, step):
        return move(value, [(c, c - 1) for c in range(1, cols + 1 - step)])

    def up(value, step):
        return move(value, [(c, c + 1) for c in range(step - 1, cols - 1)])

    padded = jnp.pad(factor_two, ((0, 0), (last * span_two, 0)))
    beside = lax.dynamic_slice(padded, (0, place * span_two), (span_two, cols * span_two))
    mix_far = beside.T.reshape(cols, span_two, span_two)[::-1]
    mix_near = jnp.stack(
        [mix_far[0]]
        + [move(mix_far[d], [(c, c - d) for c in range(d, cols)]) for d in range(1, cols)]
    )

    every = (0, span_two)
    first = flat(exchange(pack(cotangent, swap, groups[0], every, rows)))
    firsts = [first, down(first, 1)]
    far_part = pack(cotangent, swap, groups[2], every, rows)
    far_part = flat(exchange(after(far_part, first, mix_near)))
    for step in range(2, cols):
        firsts.append(down(firsts[-1], step))
    own = shares(far_part, mix_far, cuts, per)
    sums = []
    for q in range(len(cuts)):
        held = after(own[last][q], *sums)
        sums.append(move(held, [(c, c - 1) for c in range(last, cols)]))
    z_first = pack(latent, swap, (0, tiles), cuts[0], rows)
    block = cuts[0][1] * LANES
    extra = -(-factor_one.size // block)
    full_one = jnp.pad(factor_one.reshape(-1), (0, extra * block - factor_one.size))
    full_one = full_one.reshape(1, extra, cuts[0][1], LANES)
    full_one = jnp.broadcast_to(full_one, (rows,) + full_one.shape[1:])
    z_first = jnp.concatenate([z_first, full_one], axis=1)
    z_first = exchange(after(z_first, far_part, firsts[1]))
    full_one = z_first[:, tiles:].reshape(rows, -1)[:, : factor_one.size]
    z_first = z_first[:, :tiles]
    second = pack(cotangent, swap, groups[1], every, rows)
    second = flat(exchange(after(second, z_first, firsts[min(2, last)], sums[0])))

    full_one = full_one.reshape(order_one, order_one)
    spot = lax.broadcasted_iota(jnp.int32, (order_one, order_one), 0)
    target = lax.broadcasted_iota(jnp.int32, spot.shape, 1)
    unit_of, tile = spot // (rows * tiles), spot % (rows * tiles)
    pick_latent = (target == tile * fold + unit_of).astype(BF16)
    index = 0
    for lo, hi in groups:
        inside = (tile >= rows * lo) & (tile < rows * hi)
        here = tile - rows * lo
        here = here // (hi - lo) * span_one + (lo + here % (hi - lo)) * fold + unit_of
        index = jnp.where(inside, here, index)
    pick_cotan = (target == index).astype(BF16)
    left = dot_nt(dot(pick_cotan, full_one).astype(BF16), pick_latent).astype(BF16)
    left_t = left.T

    counts = [rows * (hi - lo) for lo, hi in groups]
    y_first, *v_first = raise_field(turn(flat(z_first)), left, fold, counts)
    v_first = [turn(v) for v in v_first]
    ups_first = [v_first[-1]]
    for step in range(1, cols):
        ups_first.append(up(ups_first[-1], step))
    seconds = [second, down(after(second, v_first[-1]), 1)]
    z_last = pack(latent, swap, (0, tiles), cuts[1], rows)

    def hop(q, back):
        value = sums[q] if back == last else add(sums[q], own[back][q])
        return move(value, [(c, c - 1) for c in range(back, cols)])

    later = max(last - 1, 0)
    if later:
        sums[0] = hop(0, later)
    z_last = exchange(after(z_last, second, firsts[last], sums[0]))
    z_last = after(z_last, seconds[1], sums[1])
    y_last, *v_last = raise_field(turn(flat(z_last)), left, fold, counts)
    v_last = [turn(v) for v in v_last]
    ups_last = [v_last[-1]]
    for step in range(1, cols):
        ups_last.append(up(ups_last[-1], step))
    for back in range(later - 1, 1, -1):
        sums[0] = hop(0, back)
    if later:
        sums[1] = hop(1, later)
    early = sums[1]
    for back in range(later - 1, 1, -1):
        sums[1] = hop(1, back)
    for step in range(2, cols):
        held = seconds[-1]
        if step == last:
            held = after(held, v_last[-1], ups_first[1])
        seconds.append(down(held, step))

    bits = [(0, 0, half), (0, half, unit), (1, unit, span_two)]
    ends = []
    if later > 1:
        sums = [add(sums[q], own[1][q]) for q in range(2)]
    for q, lo, hi in bits:
        held = sums[q][:, lo - cuts[q][0] : hi - cuts[q][0]]
        if later > 1:
            held = after(held, ends[0] if ends else seconds[-2])
            held = move(held, [(c, c - 1) for c in range(1, cols)])
        ends.append(held)

    def second_factor(met, sent, grad_near):
        two = [grad_near[d] + (sent[d - 1] if d else met[0]) for d in range(cols)]
        two = jnp.concatenate(two, axis=0)
        two = jnp.pad(two, ((order_two - span_two, 0), (0, 0)))
        two = lax.dynamic_slice(
            two, (order_two - span_two - place * span_two, 0), (order_two, span_two)
        )
        return two.reshape(rows, order_two // rows, span_two)

    met = [pairs(far_part, [ups_first[d], ups_last[d]], per) for d in range(cols)]
    sent = [move(met[d], [(c, c - d) for c in range(d, cols)]) for d in range(1, cols)]

    w_near, grad_near = [], 0.0
    for g, chunk in enumerate((firsts, seconds)):
        held = [chunk[0]] + chunk[1:]
        if g:
            held[0] = after(held[0], early, met[min(2, last)], ups_first[last])
        else:
            held[0] = after(held[0], met[0], met[1])
        *w, grad = gathered(held, [v_first[g], v_last[g]], mix_near, cuts, per)
        w_near.append(w)
        grad_near = grad_near + grad
    one, moved = None, []
    for n, (q, lo, hi) in enumerate(bits):
        own_here = own[0][q][:, lo - cuts[q][0] : hi - cuts[q][0]]
        share = turn(add(ends[n], own_here))
        if n == 0:
            share = after(share, ends[2])
        else:
            share = after(share, one, *sent[:2])
        parts = [turn(w[q][:, lo - cuts[q][0] : hi - cuts[q][0]]) for w in w_near] + [share]
        grad, w_y = finish(parts, left_t, fold)
        one = match(w_y, y_last if q else y_first, (lo - cuts[q][0]) // (2 * fold), one)
        grad = turn(grad).reshape(rows, tiles, hi - lo, LANES)
        if n == 2:
            grad = after(grad, ups_last[last])
        moved.append(exchange(after(grad, *moved[-1:])))

    where = [(lo, hi, half if q == 0 else unit) for q, lo, hi in bits]
    span_col = order_one // cols
    one = dot(one.astype(BF16), pick_latent).astype(BF16)
    one = jnp.transpose(one.reshape(order_one, cols, span_col), (1, 0, 2))
    total = lax.dynamic_index_in_dim(one, place, 0, keepdims=False).astype(F32)
    grad_latent = unpack(moved[0], swap, latent.shape, where[0], None)
    for d in range(1, cols):
        ring = [(c, (c + d) % cols) for c in range(cols)]
        mine = move(lax.dynamic_index_in_dim(one, (place + d) % cols, 0, keepdims=False), ring)
        if d == 1:
            mine, grad_latent = lax.optimization_barrier((mine, grad_latent))
        total = total + mine.astype(F32)
    total = total.reshape(fold, rows * tiles, span_col)
    total = jnp.concatenate(
        [
            total[:, rows * lo : rows * hi].reshape(fold, rows, hi - lo, span_col)
            for lo, hi in groups
        ],
        axis=2,
    )
    total = jnp.transpose(total, (1, 2, 0, 3)).reshape(rows, span_one, span_col)
    total = jnp.concatenate([total, second_factor(met, sent, grad_near)], axis=2)
    total = exchange(after(total, moved[2])).sum(0)
    grad_one = keep_lower(total[:, :span_col], depth)
    grad_two = keep_lower(total[:, span_col:], depth)
    for n in (1, 2):
        grad_latent = unpack(moved[n], swap, latent.shape, where[n], grad_latent)
    return (grad_latent, grad_one, grad_two)


def tiles_fit(rows, cols, span_one, span_two, depth):
    if depth % LANES or depth % rows or LANES * rows % depth:
        return False
    fold = LANES * rows // depth
    if fold > LANES or LANES % fold or depth // LANES * fold != rows:
        return False
    return (
        cols > 1
        and rows % 8 == 0
        and span_one % fold == 0
        and span_one // fold >= 4
        and span_two % (2 * fold) == 0
        and span_two % 8 == 0
        and span_two >= 64
        and 16 % (2 * fold) == 0
    )


def solution(mesh):
    rows, cols = mesh.shape["row"], mesh.shape["col"]

    def on_device(latent, cotangent, factor_one, factor_two):
        if tiles_fit(rows, cols, *latent.shape):
            return by_tiles(rows, cols, latent, cotangent, factor_one, factor_two)
        return by_lines(latent, cotangent, factor_one, factor_two)

    placed = (P("row", "col", None), P("row", "col", None), P("row", None), P("col", None))
    return jax.shard_map(
        on_device,
        mesh=mesh,
        in_specs=placed,
        out_specs=(P("row", "col", None), P("row", "col"), P("row", "col")),
        check_vma=False,
    )
```
